32 devices in a mesh: groups: 2 (over y), branch: 4 (over z), dp: 2 (over x), mp: 2 (over core).
Axes of the slice: x: 2, y: 2, z: 4, core: 2. Of those that a mesh axis runs over, the one named last changes fastest.
Arguments:
- queries: bfloat16 [4, 4, 384, 4096], P(('groups', 'dp'), 'branch', None, 'mp'), parts along dimension 0, may hold values from -160 to 160
- own_kv: bfloat16 [4, 4, 2, 384, 512], P(('groups', 'dp'), 'branch', None, None, 'mp'), parts along dimension 0, may hold values from -6 to 6
- segment_key_values: bfloat16 [4, 4, 3, 2, 128, 512], P(('groups', 'dp'), 'branch', None, None, None, 'mp'), parts along dimension 0, may hold values from -6 to 6
- ancestors: int32 [4, 4, 3], P(('groups', 'dp'), 'branch'), parts along dimension 0, may hold values from 0 to 3, as said below
- seg_tiles: int32 [4, 4, 3], P(('groups', 'dp'), 'branch'), parts along dimension 0, may hold values from 1 to 2, as said below
- grad_out: bfloat16 [4, 4, 384, 4096], P(('groups', 'dp'), 'branch', None, 'mp'), parts along dimension 0, may hold values from -6 to 6
Outputs:
- attn_out: bfloat16 [4, 4, 384, 4096], P(('groups', 'dp'), 'branch', None, 'mp'), parts along dimension 0
- d_queries: bfloat16 [4, 4, 384, 4096], P(('groups', 'dp'), 'branch', None, 'mp'), parts along dimension 0
- branch_key_value_gradient: float32 [4, 4, 2, 384, 512], P(('groups', 'dp'), 'branch', None, None, 'mp'), parts along dimension 0
- d_seg_kv: float32 [4, 4, 3, 2, 128, 512], P(('groups', 'dp'), 'branch', None, None, None, 'mp'), parts along dimension 0
The draws below stay inside these ranges and needn't reach their ends.
There are 2 independent parts, one for each index of `groups`. The reference program is written for one: setup_inputs(seed, part) draws one part's arguments, and reference() takes and returns one part's arrays. A program takes and returns all parts, laid end to end along the dimension named above; each array names one. Nothing has to cross between parts.
Inputs may be any that keep to these rules, and one draw needn't show every extreme that they name: ancestors[p, b, 0] = 0; at each level the branches with ancestor h form one contiguous run that begins at branch h, and each level's runs split those of the level before. `seg_tiles`: the segment that branch 0 stores for level 0 has 2 tiles.
All inputs are finite; a program needn't handle non-finite values.
Results may differ from the reference program's by a relative error of at most 0.035.
Values may be sent and summed in bfloat16 or wider, within the bound.
A program may use at most 128 MiB of HBM per device.

```python
import jax
import jax.numpy as jnp
from jax import lax

QUERY_HEAD_COUNT = 32
KEY_VALUE_HEADS = 4
HEAD_DIMENSION = 128
BRANCH_TOKENS = 384
TREE_LEVELS = 3
MAXT = 2
TILE = 64
SEGMENT_LENGTH = 128
N_BRANCH = 4
N_DP = 2


def shared_keys(key):
    return jnp.clip(jax.random.normal(key, (N_DP, N_BRANCH, BRANCH_TOKENS, KEY_VALUE_HEADS * HEAD_DIMENSION), jnp.float32), -6.0, 6.0)


def draw_own_kv(key, part):
    base_offset = shared_keys(key)
    key = jax.random.fold_in(key, 2)
    values = jnp.clip(jax.random.normal(key, base_offset.shape, jnp.float32), -6.0, 6.0)
    return jnp.stack([base_offset, values], axis=2).astype(jnp.bfloat16)


def draw_queries(key, part):
    key = jax.random.fold_in(key, 3)
    drawn = jnp.clip(jax.random.normal(key, (N_DP, N_BRANCH, BRANCH_TOKENS, QUERY_HEAD_COUNT * HEAD_DIMENSION), jnp.float32), -6.0, 6.0)
    return drawn.astype(jnp.bfloat16)


def draw_ancestors(key, part):
    key = jax.random.fold_in(key, 5)
    split_level = jax.random.randint(key, (N_DP, N_BRANCH), 1, TREE_LEVELS + 1)
    positions = jnp.arange(N_BRANCH, dtype=jnp.int32)
    split_level = jnp.where(positions[None, :] == N_BRANCH - 1, TREE_LEVELS - 1, split_level)
    split_level = jnp.where(positions[None, :] == 0, 0, split_level)
    levels = jnp.arange(TREE_LEVELS, dtype=jnp.int32)
    starts = split_level[:, None, :] <= levels[None, :, None]
    marked = jnp.where(starts, positions[None, None, :], 0)
    heads = lax.cummax(marked, axis=2)
    return jnp.transpose(heads, (0, 2, 1)).astype(jnp.int32)


def draw_seg_tiles(key, part):
    key = jax.random.fold_in(key, 7)
    counts = jax.random.randint(key, (N_DP, N_BRANCH, TREE_LEVELS), 1, MAXT + 1)
    return counts.at[:, 0, 0].set(MAXT).astype(jnp.int32)


def steps_of(rng, extent, pieces, least, largest):
    loudness, own = 1.0, jax.random.fold_in(rng, 6)
    for dim, shards_of in pieces:
        draws = jnp.exp(jax.random.uniform(jax.random.fold_in(own, dim), (shards_of,), jnp.float32, least / len(pieces), largest / len(pieces)))
        loudness = loudness * jnp.repeat(draws, extent[dim] // shards_of).reshape([-1 if axis == dim else 1 for axis in range(len(extent))])
    return loudness


def gaussian(stream_key, extent, width, most, cuts=(), kind=jnp.bfloat16):
    factor_of = steps_of(stream_key, extent, cuts, -0.22, 0.18) if cuts else 1.0
    values = jax.random.normal(stream_key, extent, jnp.float32) * width * factor_of
    return jnp.minimum(jnp.maximum(values, -most), most).astype(kind)


def setup_inputs(seed: int = 0, part: int = 0) -> dict:
    key_list = jax.random.split(jax.random.key(seed), 7)
    part_keys = jax.random.split(jax.random.fold_in(key_list[6], part), 7)
    return {
        "queries": draw_queries(jax.random.fold_in(jax.random.fold_in(key_list[6], part), 71), part),
        "own_kv": draw_own_kv(jax.random.fold_in(jax.random.fold_in(key_list[6], part), 71), part),
        "segment_key_values": gaussian(part_keys[2], (N_DP, N_BRANCH, TREE_LEVELS, 2, SEGMENT_LENGTH, KEY_VALUE_HEADS * HEAD_DIMENSION), 1.0, 6.0, ((0, 2), (1, 4), (5, 2))),
        "ancestors": draw_ancestors(jax.random.fold_in(jax.random.fold_in(key_list[6], part), 71), part),
        "seg_tiles": draw_seg_tiles(jax.random.fold_in(jax.random.fold_in(key_list[6], part), 71), part),
        "grad_out": gaussian(part_keys[5], (N_DP, N_BRANCH, BRANCH_TOKENS, QUERY_HEAD_COUNT * HEAD_DIMENSION), 1.0, 6.0, ((0, 2), (1, 4), (3, 2))),
    }


def attend_pair(query_row_block, gradient_row_block, every_key_row, every_value_row, allowed):
    query_group_width = QUERY_HEAD_COUNT // KEY_VALUE_HEADS
    score_scale = HEAD_DIMENSION ** -0.5
    key_position_count = every_key_row.shape[0]
    query_head_block = query_row_block.astype(jnp.float32).reshape(BRANCH_TOKENS, KEY_VALUE_HEADS, query_group_width, HEAD_DIMENSION)
    gradient_per_head = gradient_row_block.astype(jnp.float32).reshape(BRANCH_TOKENS, KEY_VALUE_HEADS, query_group_width, HEAD_DIMENSION)
    key_head_block = every_key_row.astype(jnp.float32).reshape(key_position_count, KEY_VALUE_HEADS, HEAD_DIMENSION)
    value_head_block = every_value_row.astype(jnp.float32).reshape(key_position_count, KEY_VALUE_HEADS, HEAD_DIMENSION)
    scores = jnp.einsum('qgrd,kgd->grqk', query_head_block, key_head_block) * score_scale
    scores = jnp.where(allowed[None, None], scores, -1e30)
    row_max = jnp.max(scores, axis=-1, keepdims=True)
    weights = jnp.exp(scores - row_max)
    probabilities = weights / jnp.sum(weights, axis=-1, keepdims=True)
    probs_b = lax.optimization_barrier(probabilities.astype(jnp.bfloat16)).astype(jnp.float32)
    output = jnp.einsum('grqk,kgd->qgrd', probs_b, value_head_block).astype(jnp.bfloat16)
    row_delta = jnp.sum(gradient_per_head * output.astype(jnp.float32), axis=-1)
    grad_probs = jnp.einsum('qgrd,kgd->grqk', gradient_per_head, value_head_block)
    grad_scores = probabilities * (grad_probs - jnp.transpose(row_delta, (1, 2, 0))[..., None])
    scores_b = lax.optimization_barrier(grad_scores.astype(jnp.bfloat16)).astype(jnp.float32)
    grad_query = (jnp.einsum('grqk,kgd->qgrd', scores_b, key_head_block) * score_scale).astype(jnp.bfloat16)
    key_gradient = jnp.einsum('grqk,qgrd->kgd', scores_b, query_head_block) * score_scale
    value_gradient = jnp.einsum('grqk,qgrd->kgd', probs_b, gradient_per_head)
    return (output.reshape(BRANCH_TOKENS, QUERY_HEAD_COUNT * HEAD_DIMENSION), grad_query.reshape(BRANCH_TOKENS, QUERY_HEAD_COUNT * HEAD_DIMENSION),
            key_gradient.reshape(key_position_count, KEY_VALUE_HEADS * HEAD_DIMENSION), value_gradient.reshape(key_position_count, KEY_VALUE_HEADS * HEAD_DIMENSION))


def reference(queries, own_kv, segment_key_values, ancestors, seg_tiles, grad_out):
    pair_count = N_DP * N_BRANCH
    shared_prefix_length = TREE_LEVELS * SEGMENT_LENGTH

    def one_pair(pair_index):
        prompt = pair_index // N_BRANCH
        branch = pair_index % N_BRANCH
        lineage = ancestors[prompt, branch]
        key_parts = []
        value_parts = []
        valid_parts = []
        for depth_level in range(TREE_LEVELS):
            holder = lineage[depth_level]
            stored = segment_key_values[prompt, holder, depth_level]
            key_parts.append(stored[0])
            value_parts.append(stored[1])
            limit = seg_tiles[prompt, holder, depth_level] * TILE
            valid_parts.append(jnp.arange(SEGMENT_LENGTH) < limit)
        own_pair = own_kv[prompt, branch]
        every_key_row = jnp.concatenate(key_parts + [own_pair[0]], axis=0)
        every_value_row = jnp.concatenate(value_parts + [own_pair[1]], axis=0)
        prefix_ok = jnp.concatenate(valid_parts, axis=0)
        own_rows = jnp.arange(BRANCH_TOKENS)
        causal = own_rows[None, :] <= own_rows[:, None]
        allowed = jnp.concatenate([jnp.broadcast_to(prefix_ok[None, :], (BRANCH_TOKENS, shared_prefix_length)), causal], axis=1)
        output, grad_query, key_gradient, value_gradient = attend_pair(
            queries[prompt, branch], grad_out[prompt, branch], every_key_row, every_value_row, allowed)
        own_grad = jnp.stack([key_gradient[shared_prefix_length:], value_gradient[shared_prefix_length:]], axis=0)
        shared_prefix_gradient = jnp.stack([key_gradient[:shared_prefix_length].reshape(TREE_LEVELS, SEGMENT_LENGTH, KEY_VALUE_HEADS * HEAD_DIMENSION),
                                 value_gradient[:shared_prefix_length].reshape(TREE_LEVELS, SEGMENT_LENGTH, KEY_VALUE_HEADS * HEAD_DIMENSION)], axis=1).astype(jnp.bfloat16)
        return output, grad_query, own_grad, shared_prefix_gradient

    outputs, grad_queries, branch_gradients, prefix_grads = lax.map(one_pair, jnp.arange(pair_count))
    prompt_ids = jnp.arange(pair_count) // N_BRANCH
    holders = ancestors.reshape(pair_count, TREE_LEVELS)
    segment_total_length = jnp.zeros((N_DP, N_BRANCH, TREE_LEVELS, 2, SEGMENT_LENGTH, KEY_VALUE_HEADS * HEAD_DIMENSION), jnp.float32)
    for depth_level in range(TREE_LEVELS):
        segment_total_length = segment_total_length.at[prompt_ids, holders[:, depth_level], depth_level].add(
            prefix_grads[:, depth_level].astype(jnp.float32))
    attn_out = outputs.reshape(N_DP, N_BRANCH, BRANCH_TOKENS, QUERY_HEAD_COUNT * HEAD_DIMENSION)
    d_queries = grad_queries.reshape(N_DP, N_BRANCH, BRANCH_TOKENS, QUERY_HEAD_COUNT * HEAD_DIMENSION)
    branch_key_value_gradient = branch_gradients.reshape(N_DP, N_BRANCH, 2, BRANCH_TOKENS, KEY_VALUE_HEADS * HEAD_DIMENSION)
    return attn_out, d_queries, branch_key_value_gradient, segment_total_length
```

```python
import functools
import math

import jax
import jax.numpy as jnp
from jax import lax
from jax.experimental import pallas as pl
from jax.experimental.pallas import tpu as pltpu
from jax.sharding import PartitionSpec as P

QUERY_HEAD_COUNT = 32
KEY_VALUE_HEADS = 4
D = 128
TILE = 64
GROUP = QUERY_HEAD_COUNT // KEY_VALUE_HEADS
SCALE = D ** (-0.5)
LOG2E = 1.0 / math.log(2.0)
MESH = pl.DeviceIdType.MESH
NEG = -1e30
COUNT_ROWS = 16


def kernel(
    n,
    q_hbm,
    do_hbm,
    own_ref,
    seg_ref,
    anc_ref,
    tiles_ref,
    o_hbm,
    dq_hbm,
    down_ref,
    dseg_ref,
    q_v,
    do_v,
    o_v,
    dq_v,
    cur,
    recv,
    gsend,
    grecv,
    k_all,
    v_all,
    k_t,
    v_t,
    acc_k,
    acc_v,
    in_sem,
    out_sem,
    send_sem,
    recv_sem,
    gsend_sem,
    grecv_sem,
):
    levels, seg_len = seg_ref.shape[0], seg_ref.shape[2]
    heads = seg_ref.shape[3] // D
    own_len = own_ref.shape[1]
    pre = levels * seg_len
    width = GROUP * D
    me = lax.axis_index("branch")
    right, left = me + 1, me - 1

    in_copies = []
    for h in range(heads):
        cols = pl.ds(h * width, width)
        for i, (src, dst) in enumerate(((q_hbm, q_v), (do_hbm, do_v))):
            copy = pltpu.make_async_copy(src.at[:, cols], dst.at[:, cols], in_sem.at[h, i])
            copy.start()
            in_copies.append(copy)

    barrier = pltpu.get_barrier_semaphore()

    @pl.when(me > 0)
    def _():
        pl.semaphore_signal(barrier, inc=1, device_id={"branch": left}, device_id_type=MESH)

    @pl.when(me < n - 1)
    def _():
        pl.semaphore_signal(barrier, inc=1, device_id={"branch": right}, device_id_type=MESH)

    @pl.when((me == 0) | (me == n - 1))
    def _():
        pl.semaphore_wait(barrier, 1)

    @pl.when((me > 0) & (me < n - 1))
    def _():
        pl.semaphore_wait(barrier, 2)

    def down_copy(h, l):
        return pltpu.make_async_remote_copy(
            src_ref=cur.at[h, l],
            dst_ref=recv.at[h, l],
            send_sem=send_sem.at[h, l],
            recv_sem=recv_sem.at[h, l],
            device_id={"branch": right},
            device_id_type=MESH,
        )

    def up_copy(h, l):
        return pltpu.make_async_remote_copy(
            src_ref=gsend.at[h, l],
            dst_ref=grecv.at[h, l],
            send_sem=gsend_sem.at[h, l],
            recv_sem=grecv_sem.at[h, l],
            device_id={"branch": left},
            device_id_type=MESH,
        )

    def take_prefix(h):
        cols = slice(h * D, (h + 1) * D)
        for l in range(levels):
            count = jnp.full((COUNT_ROWS, D), tiles_ref[0, 0, l].astype(jnp.float32)).astype(jnp.bfloat16)
            stored = jnp.concatenate([seg_ref[l, 0, :, cols], seg_ref[l, 1, :, cols], count], axis=0)

            @pl.when(me == 0)
            def _():
                cur[h, l] = stored

            @pl.when(me > 0)
            def _():
                down_copy(h, l).wait_recv()
                mine = anc_ref[0, 0, l] == me
                cur[h, l] = jnp.where(mine, stored, recv[h, l])

            @pl.when(me < n - 1)
            def _():
                down_copy(h, l).start()

    def load_own(h):
        cols = slice(h * D, (h + 1) * D)
        k_all[pre:, :] = own_ref[0, :, cols]
        v_all[pre:, :] = own_ref[1, :, cols]
        k_t[:, pre:] = own_ref[0, :, cols].T
        v_t[:, pre:] = own_ref[1, :, cols].T
        acc_k[...] = jnp.zeros_like(acc_k)
        acc_v[...] = jnp.zeros_like(acc_v)

    def load_prefix(h):
        for l in range(levels):
            rows = slice(l * seg_len, (l + 1) * seg_len)
            k = cur[h, l, 0:seg_len, :]
            v = cur[h, l, seg_len : 2 * seg_len, :]
            k_all[rows, :] = k
            v_all[rows, :] = v
            k_t[:, rows] = k.T
            v_t[:, rows] = v.T

    def run_block(h, b, bias):
        rows = slice(b * D, (b + 1) * D)
        nk = pre + (b + 1) * D
        key_at = lax.broadcasted_iota(jnp.int32, (D, 2 * D), 0)
        query_at = lax.broadcasted_iota(jnp.int32, (D, 2 * D), 1)
        visible = key_at <= jnp.where(query_at >= D, query_at - D, query_at)

        def pair(j, carry):
            first = pl.ds(pl.multiple_of(h * width + j * (2 * D), D), D)
            second = pl.ds(pl.multiple_of(h * width + j * (2 * D) + D, D), D)
            qs = jnp.concatenate([q_v[rows, first], q_v[rows, second]], axis=0)
            gs = jnp.concatenate([do_v[rows, first], do_v[rows, second]], axis=0)
            nt = (((1,), (1,)), ((), ()))
            s = lax.dot_general(k_all[0:nk, :], qs, nt, preferred_element_type=jnp.float32)
            parts = []
            for l in range(levels):
                for t in range(seg_len // TILE):
                    lo = l * seg_len + t * TILE
                    part = s[lo : lo + TILE]
                    if t:
                        part = part + bias[l][t - 1]
                    parts.append(part)
            if b:
                parts.append(s[pre : nk - D])
            parts.append(jnp.where(visible, s[nk - D : nk], NEG))
            s = jnp.concatenate(parts, axis=0)
            m = jnp.max(s, axis=0, keepdims=True)
            w = jnp.exp2((s - m) * (SCALE * LOG2E))
            rl = 1.0 / jnp.sum(w, axis=0, keepdims=True)
            o_t = jnp.dot(v_t[:, 0:nk], w.astype(jnp.bfloat16), preferred_element_type=jnp.float32) * rl
            dp = lax.dot_general(v_all[0:nk, :], gs, nt, preferred_element_type=jnp.float32)
            delta = jnp.sum(gs.T.astype(jnp.float32) * o_t, axis=0, keepdims=True)
            p = w * rl
            ds = (p * (dp - delta)).astype(jnp.bfloat16)
            acc_v[0:nk, :] += jnp.dot(p.astype(jnp.bfloat16), gs, preferred_element_type=jnp.float32)
            acc_k[0:nk, :] += jnp.dot(ds, qs, preferred_element_type=jnp.float32)
            dq_t = jnp.dot(k_t[:, 0:nk], ds, preferred_element_type=jnp.float32) * SCALE
            o = o_t.astype(jnp.bfloat16).T
            dq = dq_t.astype(jnp.bfloat16).T
            o_v[rows, first] = o[0:D]
            o_v[rows, second] = o[D : 2 * D]
            dq_v[rows, first] = dq[0:D]
            dq_v[rows, second] = dq[D : 2 * D]
            return carry

        lax.fori_loop(0, GROUP // 2, pair, 0)

    def bias_of(h):
        out = []
        for l in range(levels):
            count = cur[h, l, 2 * seg_len : 2 * seg_len + COUNT_ROWS, :].astype(jnp.float32)[0:1, :]
            count = jnp.concatenate([count, count], axis=1)
            out.append([jnp.where(count > t + 0.5, 0.0, NEG) for t in range(1, seg_len // TILE)])
        return out

    def own_grads(h):
        cols = slice(h * D, (h + 1) * D)
        down_ref[0, :, cols] = acc_k[pre:, :] * SCALE
        down_ref[1, :, cols] = acc_v[pre:, :]

    def stage_grads(h):
        for l in range(levels):
            rows = slice(l * seg_len, (l + 1) * seg_len)
            gsend[h, l, 0:seg_len, :] = (acc_k[rows, :] * SCALE).astype(jnp.bfloat16)
            gsend[h, l, seg_len:, :] = acc_v[rows, :].astype(jnp.bfloat16)

    def pass_grads(h):
        cols = slice(h * D, (h + 1) * D)
        for l in range(levels):
            mine = anc_ref[0, 0, l] == me

            def finish(total):
                kept = jnp.where(mine, total, 0.0)
                dseg_ref[l, 0, :, cols] = kept[0:seg_len]
                dseg_ref[l, 1, :, cols] = kept[seg_len:]
                gsend[h, l] = jnp.where(mine, 0.0, total).astype(jnp.bfloat16)

            @pl.when(me == n - 1)
            def _():
                finish(gsend[h, l].astype(jnp.float32))

            @pl.when(me < n - 1)
            def _():
                up_copy(h, l).wait_recv()
                finish(gsend[h, l].astype(jnp.float32) + grecv[h, l].astype(jnp.float32))

            @pl.when(me > 0)
            def _():
                up_copy(h, l).start()

    out_copies = []

    def write_out(h):
        cols = pl.ds(h * width, width)
        for i, (src, dst) in enumerate(((o_v, o_hbm), (dq_v, dq_hbm))):
            copy = pltpu.make_async_copy(src.at[:, cols], dst.at[:, cols], out_sem.at[h, i])
            copy.start()
            out_copies.append(copy)

    blocks = own_len // D
    for h in range(heads):
        if h == 0:
            take_prefix(0)
        load_own(h)
        load_prefix(h)
        in_copies[2 * h].wait()
        in_copies[2 * h + 1].wait()
        bias = bias_of(h)
        for b in range(blocks):
            run_block(h, b, bias)
            if b == 0 and h + 1 < heads:
                take_prefix(h + 1)
            if h > 0:
                stage = n - 2 - b

                @pl.when((me == stage) if b < blocks - 1 else (me <= stage))
                def _():
                    pass_grads(h - 1)

        write_out(h)
        stage_grads(h)
        if h + 1 < heads:

            @pl.when(me == n - 1)
            def _():
                pass_grads(h)

        own_grads(h)
    pass_grads(heads - 1)

    for copy in out_copies:
        copy.wait()

    @pl.when(me < n - 1)
    def _():
        for h in range(heads):
            for l in range(levels):
                down_copy(h, l).wait_send()

    @pl.when(me > 0)
    def _():
        for h in range(heads):
            for l in range(levels):
                up_copy(h, l).wait_send()


def local(n, queries, own_kv, segment_key_values, ancestors, seg_tiles, grad_out):
    own_len, q_width = queries.shape[2:]
    levels, _, seg_len, kv_width = segment_key_values.shape[2:]
    heads = kv_width // D
    keys = levels * seg_len + own_len
    vmem = pl.BlockSpec(memory_space=pltpu.VMEM)
    smem = pl.BlockSpec(memory_space=pltpu.SMEM)
    hbm = pl.BlockSpec(memory_space=pl.ANY)
    bf16, f32 = jnp.bfloat16, jnp.float32
    rows_of = pltpu.VMEM((own_len, q_width), bf16)
    out = pl.pallas_call(
        functools.partial(kernel, n),
        out_shape=(
            jax.ShapeDtypeStruct((own_len, q_width), bf16),
            jax.ShapeDtypeStruct((own_len, q_width), bf16),
            jax.ShapeDtypeStruct((2, own_len, kv_width), f32),
            jax.ShapeDtypeStruct((levels, 2, seg_len, kv_width), f32),
        ),
        in_specs=[hbm, hbm, vmem, vmem, smem, smem],
        out_specs=(hbm, hbm, vmem, vmem),
        scratch_shapes=[
            rows_of,
            rows_of,
            rows_of,
            rows_of,
            pltpu.VMEM((heads, levels, 2 * seg_len + COUNT_ROWS, D), bf16),
            pltpu.VMEM((heads, levels, 2 * seg_len + COUNT_ROWS, D), bf16),
            pltpu.VMEM((heads, levels, 2 * seg_len, D), bf16),
            pltpu.VMEM((heads, levels, 2 * seg_len, D), bf16),
            pltpu.VMEM((keys, D), bf16),
            pltpu.VMEM((keys, D), bf16),
            pltpu.VMEM((D, keys), bf16),
            pltpu.VMEM((D, keys), bf16),
            pltpu.VMEM((keys, D), f32),
            pltpu.VMEM((keys, D), f32),
            pltpu.SemaphoreType.DMA((heads, 2)),
            pltpu.SemaphoreType.DMA((heads, 2)),
            pltpu.SemaphoreType.DMA((heads, levels)),
            pltpu.SemaphoreType.DMA((heads, levels)),
            pltpu.SemaphoreType.DMA((heads, levels)),
            pltpu.SemaphoreType.DMA((heads, levels)),
        ],
        compiler_params=pltpu.CompilerParams(
            collective_id=0, has_side_effects=True, vmem_limit_bytes=48 * 1024 * 1024
        ),
    )(queries[0, 0], grad_out[0, 0], own_kv[0, 0], segment_key_values[0, 0], ancestors, seg_tiles)
    return tuple(x[None, None] for x in out)


def solution(mesh):
    placed = (
        P(("groups", "dp"), "branch", None, "mp"),
        P(("groups", "dp"), "branch", None, None, "mp"),
        P(("groups", "dp"), "branch", None, None, None, "mp"),
        P(("groups", "dp"), "branch", None),
        P(("groups", "dp"), "branch", None),
        P(("groups", "dp"), "branch", None, "mp"),
    )
    return jax.shard_map(
        functools.partial(local, mesh.shape["branch"]),
        mesh=mesh,
        in_specs=placed,
        out_specs=(
            P(("groups", "dp"), "branch", None, "mp"),
            P(("groups", "dp"), "branch", None, "mp"),
            P(("groups", "dp"), "branch", None, None, "mp"),
            P(("groups", "dp"), "branch", None, None, None, "mp"),
        ),
        check_vma=False,
    )
```

```python
import functools
import math

import jax
import jax.numpy as jnp
from jax import lax
from jax.experimental import pallas as pl
from jax.experimental.pallas import tpu as pltpu
from jax.sharding import PartitionSpec as P

QUERY_HEAD_COUNT = 32
KEY_VALUE_HEADS = 4
D = 128
TILE = 64
GROUP = QUERY_HEAD_COUNT // KEY_VALUE_HEADS
SCALE = D ** (-0.5)
LOG2E = 1.0 / math.log(2.0)
MESH = pl.DeviceIdType.MESH
NEG = -1e30
COUNT_ROWS = 16


def kernel(
    n,
    q_hbm,
    do_hbm,
    own_hbm,
    seg_hbm,
    anc_hbm,
    tiles_hbm,
    o_hbm,
    dq_hbm,
    down_ref,
    dseg_ref,
    q_v,
    do_v,
    o_v,
    dq_v,
    own_ref,
    seg_ref,
    anc_ref,
    tiles_ref,
    cur,
    recv,
    gsend,
    grecv,
    k_all,
    v_all,
    k_t,
    v_t,
    acc_k,
    acc_v,
    small_sem,
    in_sem,
    out_sem,
    send_sem,
    recv_sem,
    gsend_sem,
    grecv_sem,
):
    levels, seg_len = seg_ref.shape[0], seg_ref.shape[2]
    heads = seg_ref.shape[3] // D
    own_len = own_ref.shape[1]
    pre = levels * seg_len
    width = GROUP * D
    me = lax.axis_index("branch")
    right, left = me + 1, me - 1

    small = []
    for i, (src, dst) in enumerate(
        ((anc_hbm, anc_ref), (tiles_hbm, tiles_ref), (seg_hbm, seg_ref), (own_hbm, own_ref))
    ):
        copy = pltpu.make_async_copy(src, dst, small_sem.at[i])
        copy.start()
        small.append(copy)
    in_copies = []
    for h in range(heads):
        cols = pl.ds(h * width, width)
        for i, (src, dst) in enumerate(((q_hbm, q_v), (do_hbm, do_v))):
            copy = pltpu.make_async_copy(src.at[:, cols], dst.at[:, cols], in_sem.at[h, i])
            copy.start()
            in_copies.append(copy)

    barrier = pltpu.get_barrier_semaphore()

    @pl.when(me > 0)
    def _():
        pl.semaphore_signal(barrier, inc=1, device_id={"branch": left}, device_id_type=MESH)

    @pl.when(me < n - 1)
    def _():
        pl.semaphore_signal(barrier, inc=1, device_id={"branch": right}, device_id_type=MESH)

    @pl.when((me == 0) | (me == n - 1))
    def _():
        pl.semaphore_wait(barrier, 1)

    @pl.when((me > 0) & (me < n - 1))
    def _():
        pl.semaphore_wait(barrier, 2)

    def down_copy(h, l, c):
        return pltpu.make_async_remote_copy(
            src_ref=cur.at[h, l, c],
            dst_ref=recv.at[h, l, c],
            send_sem=send_sem.at[h, l, c],
            recv_sem=recv_sem.at[h, l, c],
            device_id={"branch": right},
            device_id_type=MESH,
        )

    def up_copy(h, l, c):
        return pltpu.make_async_remote_copy(
            src_ref=gsend.at[h, l, c],
            dst_ref=grecv.at[h, l, c],
            send_sem=gsend_sem.at[h, l, c],
            recv_sem=grecv_sem.at[h, l, c],
            device_id={"branch": left},
            device_id_type=MESH,
        )

    def first_prefix(h):
        cols = slice(h * D, (h + 1) * D)

        @pl.when(me == 0)
        def _():
            for c in range(2):
                for l in range(levels):
                    cur[h, l, c] = stored_of(l, c, cols)
                    down_copy(h, l, c).start()

    def stored_of(l, c, cols):
        count = jnp.full((COUNT_ROWS, D), tiles_ref[0, 0, l].astype(jnp.float32)).astype(jnp.bfloat16)
        return jnp.concatenate([seg_ref[l, c, :, cols], count], axis=0)

    def take_prefix(h, c):
        cols = slice(h * D, (h + 1) * D)
        for l in range(levels):

            @pl.when(me > 0)
            def _():
                down_copy(h, l, c).wait_recv()
                mine = anc_ref[0, 0, l] == me
                cur[h, l, c] = jnp.where(mine, stored_of(l, c, cols), recv[h, l, c])

            @pl.when((me > 0) & (me < n - 1))
            def _():
                down_copy(h, l, c).start()

    def load_own(h):
        cols = slice(h * D, (h + 1) * D)
        k_all[pre:, :] = own_ref[0, :, cols]
        v_all[pre:, :] = own_ref[1, :, cols]
        k_t[:, pre:] = own_ref[0, :, cols].T
        v_t[:, pre:] = own_ref[1, :, cols].T
        acc_k[...] = jnp.zeros_like(acc_k)
        acc_v[...] = jnp.zeros_like(acc_v)

    def load_prefix(h, c):
        rows_ref, turned_ref = ((k_all, k_t), (v_all, v_t))[c]
        for l in range(levels):
            rows = slice(l * seg_len, (l + 1) * seg_len)
            x = cur[h, l, c, 0:seg_len, :]
            rows_ref[rows, :] = x
            turned_ref[:, rows] = x.T

    nt = (((1,), (1,)), ((), ()))
    key_at = lax.broadcasted_iota(jnp.int32, (D, D), 0)
    query_at = lax.broadcasted_iota(jnp.int32, (D, D), 1)
    unseen = jnp.where(key_at <= query_at, 0.0, NEG)
    unseen = jnp.concatenate([unseen] * GROUP, axis=1)

    def operands(h, b):
        rows = slice(b * D, (b + 1) * D)
        cols = [slice(h * width + i * D, h * width + (i + 1) * D) for i in range(GROUP)]
        qs = jnp.concatenate([q_v[rows, c] for c in cols], axis=0)
        gs = jnp.concatenate([do_v[rows, c] for c in cols], axis=0)
        return rows, cols, qs, gs

    def own_scores(h, b):
        _, _, qs, gs = operands(h, b)
        nk = pre + (b + 1) * D
        s = lax.dot_general(k_all[pre:nk, :], qs, nt, preferred_element_type=jnp.float32)
        diagonal = s[b * D :] + unseen
        s = jnp.concatenate([s[: b * D], diagonal], axis=0) if b else diagonal
        dp = lax.dot_general(v_all[pre:nk, :], gs, nt, preferred_element_type=jnp.float32)
        return s, dp

    def prefix_scores(h, b, bias):
        _, _, qs, _ = operands(h, b)
        s = lax.dot_general(k_all[0:pre, :], qs, nt, preferred_element_type=jnp.float32)
        parts = []
        for l in range(levels):
            for t in range(seg_len // TILE):
                lo = l * seg_len + t * TILE
                part = s[lo : lo + TILE]
                parts.append(part + bias[l][t - 1] if t else part)
        return jnp.concatenate(parts, axis=0)

    def run_block(h, b, prefix_s, own_part):
        rows, cols, qs, gs = operands(h, b)
        nk = pre + (b + 1) * D
        own_s, own_dp = own_part
        s = jnp.concatenate([prefix_s, own_s], axis=0)
        m = jnp.max(s, axis=0, keepdims=True)
        w = jnp.exp2((s - m) * (SCALE * LOG2E))
        rl = 1.0 / jnp.sum(w, axis=0, keepdims=True)
        o_t = jnp.dot(v_t[:, 0:nk], w.astype(jnp.bfloat16), preferred_element_type=jnp.float32) * rl
        dp = lax.dot_general(v_all[0:pre, :], gs, nt, preferred_element_type=jnp.float32)
        dp = jnp.concatenate([dp, own_dp], axis=0)
        delta = jnp.sum(gs.T.astype(jnp.float32) * o_t, axis=0, keepdims=True)
        p = w * rl
        ds = (p * (dp - delta)).astype(jnp.bfloat16)
        pb = p.astype(jnp.bfloat16)
        acc_v[0:pre, :] += jnp.dot(pb[0:pre], gs, preferred_element_type=jnp.float32)
        acc_k[0:pre, :] += jnp.dot(ds[0:pre], qs, preferred_element_type=jnp.float32)
        o = o_t.astype(jnp.bfloat16).T
        for i, c in enumerate(cols):
            o_v[rows, c] = o[i * D : (i + 1) * D]

        def rest():
            _, _, qs, gs = operands(h, b)
            acc_v[pre:nk, :] += jnp.dot(pb[pre:], gs, preferred_element_type=jnp.float32)
            acc_k[pre:nk, :] += jnp.dot(ds[pre:], qs, preferred_element_type=jnp.float32)
            dq_t = jnp.dot(k_t[:, 0:nk], ds, preferred_element_type=jnp.float32) * SCALE
            dq = dq_t.astype(jnp.bfloat16).T
            for i, c in enumerate(cols):
                dq_v[rows, c] = dq[i * D : (i + 1) * D]

        return rest

    def bias_of(h):
        out = []
        for l in range(levels):
            count = cur[h, l, 0, seg_len : seg_len + COUNT_ROWS, :].astype(jnp.float32)[0:1, :]
            count = jnp.concatenate([count] * GROUP, axis=1)
            out.append([jnp.where(count > t + 0.5, 0.0, NEG) for t in range(1, seg_len // TILE)])
        return out

    def own_grads(h):
        cols = slice(h * D, (h + 1) * D)
        down_ref[0, :, cols] = acc_k[pre:, :] * SCALE
        down_ref[1, :, cols] = acc_v[pre:, :]

    def pass_grads(h):
        cols = slice(h * D, (h + 1) * D)
        for l in range(levels):
            mine = anc_ref[0, 0, l] == me
            for c in range(2):

                def finish(total):
                    dseg_ref[l, c, :, cols] = jnp.where(mine, total, 0.0)
                    gsend[h, l, c] = jnp.where(mine, 0.0, total).astype(jnp.bfloat16)

                @pl.when(me == n - 1)
                def _():
                    finish(gsend[h, l, c].astype(jnp.float32))

                @pl.when(me < n - 1)
                def _():
                    up_copy(h, l, c).wait_recv()
                    finish(gsend[h, l, c].astype(jnp.float32) + grecv[h, l, c].astype(jnp.float32))

                @pl.when(me > 0)
                def _():
                    up_copy(h, l, c).start()

    def stage_grads(h):
        for l in range(levels):
            rows = slice(l * seg_len, (l + 1) * seg_len)
            gsend[h, l, 0] = (acc_k[rows, :] * SCALE).astype(jnp.bfloat16)
            gsend[h, l, 1] = acc_v[rows, :].astype(jnp.bfloat16)

        @pl.when(me == n - 1)
        def _():
            pass_grads(h)

    out_copies = []

    def write_out(h, i):
        cols = pl.ds(h * width, width)
        src, dst = ((o_v, o_hbm), (dq_v, dq_hbm))[i]
        copy = pltpu.make_async_copy(src.at[:, cols], dst.at[:, cols], out_sem.at[h, i])
        copy.start()
        out_copies.append(copy)

    blocks = own_len // D
    for copy in small:
        copy.wait()
    for h in range(heads):
        first_prefix(h)
    for h in range(heads):
        last = h == heads - 1
        load_own(h)
        in_copies[2 * h].wait()
        in_copies[2 * h + 1].wait()
        own_parts = [own_scores(h, b) for b in range(blocks)]
        if h == 0:
            take_prefix(0, 0)
        load_prefix(h, 0)
        bias = bias_of(h)
        prefix_parts = [prefix_scores(h, b, bias) for b in range(blocks)]
        if h == 0:
            take_prefix(0, 1)
        load_prefix(h, 1)
        rests = []
        for b in range(blocks):
            rests.append(run_block(h, b, prefix_parts[b], own_parts[b]))
            if not last:
                rests.pop()()
            if b == 0 and not last:
                take_prefix(h + 1, 0)
                take_prefix(h + 1, 1)
            if b == 1 and h > 0:

                @pl.when(me == n - 2)
                def _():
                    pass_grads(h - 1)

        stage_grads(h)
        write_out(h, 0)
        for rest in rests:
            rest()
        write_out(h, 1)
        own_grads(h)

    @pl.when(me < n - 2)
    def _():
        for h in range(heads - 1):
            pass_grads(h)

    @pl.when(me < n - 1)
    def _():
        pass_grads(heads - 1)

    for copy in out_copies:
        copy.wait()

    pieces = [(h, l, c) for h in range(heads) for l in range(levels) for c in range(2)]

    @pl.when(me < n - 1)
    def _():
        for piece in pieces:
            down_copy(*piece).wait_send()

    @pl.when(me > 0)
    def _():
        for piece in pieces:
            up_copy(*piece).wait_send()


def local(n, queries, own_kv, segment_key_values, ancestors, seg_tiles, grad_out):
    own_len, q_width = queries.shape[2:]
    levels, _, seg_len, kv_width = segment_key_values.shape[2:]
    heads = kv_width // D
    keys = levels * seg_len + own_len
    vmem = pl.BlockSpec(memory_space=pltpu.VMEM)
    hbm = pl.BlockSpec(memory_space=pl.ANY)
    bf16, f32 = jnp.bfloat16, jnp.float32
    rows_of = pltpu.VMEM((own_len, q_width), bf16)
    out = pl.pallas_call(
        functools.partial(kernel, n),
        out_shape=(
            jax.ShapeDtypeStruct((own_len, q_width), bf16),
            jax.ShapeDtypeStruct((own_len, q_width), bf16),
            jax.ShapeDtypeStruct((2, own_len, kv_width), f32),
            jax.ShapeDtypeStruct((levels, 2, seg_len, kv_width), f32),
        ),
        in_specs=[pl.BlockSpec(memory_space=pltpu.HBM)] * 6,
        out_specs=(hbm, hbm, vmem, vmem),
        scratch_shapes=[
            rows_of,
            rows_of,
            rows_of,
            rows_of,
            pltpu.VMEM((2, own_len, kv_width), bf16),
            pltpu.VMEM((levels, 2, seg_len, kv_width), bf16),
            pltpu.SMEM((1, 1, levels), jnp.int32),
            pltpu.SMEM((1, 1, levels), jnp.int32),
            pltpu.VMEM((heads, levels, 2, seg_len + COUNT_ROWS, D), bf16),
            pltpu.VMEM((heads, levels, 2, seg_len + COUNT_ROWS, D), bf16),
            pltpu.VMEM((heads, levels, 2, seg_len, D), bf16),
            pltpu.VMEM((heads, levels, 2, seg_len, D), bf16),
            pltpu.VMEM((keys, D), bf16),
            pltpu.VMEM((keys, D), bf16),
            pltpu.VMEM((D, keys), bf16),
            pltpu.VMEM((D, keys), bf16),
            pltpu.VMEM((keys, D), f32),
            pltpu.VMEM((keys, D), f32),
            pltpu.SemaphoreType.DMA((4,)),
            pltpu.SemaphoreType.DMA((heads, 2)),
            pltpu.SemaphoreType.DMA((heads, 2)),
            pltpu.SemaphoreType.DMA((heads, levels, 2)),
            pltpu.SemaphoreType.DMA((heads, levels, 2)),
            pltpu.SemaphoreType.DMA((heads, levels, 2)),
            pltpu.SemaphoreType.DMA((heads, levels, 2)),
        ],
        compiler_params=pltpu.CompilerParams(
            collective_id=0, has_side_effects=True, vmem_limit_bytes=48 * 1024 * 1024
        ),
    )(queries[0, 0], grad_out[0, 0], own_kv[0, 0], segment_key_values[0, 0], ancestors, seg_tiles)
    return tuple(x[None, None] for x in out)


def solution(mesh):
    placed = (
        P(("groups", "dp"), "branch", None, "mp"),
        P(("groups", "dp"), "branch", None, None, "mp"),
        P(("groups", "dp"), "branch", None, None, None, "mp"),
        P(("groups", "dp"), "branch", None),
        P(("groups", "dp"), "branch", None),
        P(("groups", "dp"), "branch", None, "mp"),
    )
    return jax.shard_map(
        functools.partial(local, mesh.shape["branch"]),
        mesh=mesh,
        in_specs=placed,
        out_specs=(
            P(("groups", "dp"), "branch", None, "mp"),
            P(("groups", "dp"), "branch", None, "mp"),
            P(("groups", "dp"), "branch", None, None, "mp"),
            P(("groups", "dp"), "branch", None, None, None, "mp"),
        ),
        check_vma=False,
    )
```
